32 devices in a mesh: grp: 2 (over x), feat: 4 (over y, core), hid: 4 (over z).
Axes of the slice: x: 2, y: 2, z: 4, core: 2. Of those that a mesh axis runs over, the one named last changes fastest.
Arguments:
- decoder: bfloat16 [32768, 4096], P(('grp', 'feat'), 'hid'), parts along dimension 0, may hold values from -6 to 6
- encoder: bfloat16 [4096, 32768], P('hid', ('grp', 'feat')), parts along dimension 1, may hold values from -0.09375 to 0.09375
- panel_rows: int32 [8, 4, 4], P(('grp', 'feat')), parts along dimension 0, may hold values from 0 to 31, as said below
- pair_panel: int32 [8, 4, 10], P(('grp', 'feat')), parts along dimension 0, may hold values from 0 to 3
- pair_cols: int32 [8, 4, 10], P(('grp', 'feat')), parts along dimension 0, may hold values from 0 to 31, as said below
- pair_counts: int32 [8, 4], P(('grp', 'feat')), parts along dimension 0, may hold values from 3 to 10, as said below
Outputs:
- virtual_blocks: float32 [320, 128, 128], P(('grp', 'feat', 'hid')), parts along dimension 0
The draws below stay inside these ranges and needn't reach their ends.
There are 2 independent parts, one for each index of `grp`. The reference program is written for one: setup_inputs(seed, part) draws one part's arguments, and reference() takes and returns one part's arrays. A program takes and returns all parts, laid end to end along the dimension named above; each array names one. Nothing has to cross between parts.
Inputs may be any that keep to these rules, and one draw needn't show every extreme that they name: `panel_rows`: within one group (d, s) the 4 entries are different. `pair_cols`: within one group (d, s) the 10 entries are different. `pair_counts`: every column shard d has some group with all 10 slots live.
All inputs are finite; a program needn't handle non-finite values.
Results may differ from the reference program's by a relative error of at most 0.0003.
Values may be sent and summed in bfloat16 or wider, within the bound.
A program may use at most 192 MiB of HBM per device.

```python
import jax
import jax.numpy as jnp
from jax import lax

H = 4096
BLK = 128
NB_DEV = 32
PPS = 10
CAP = 4
FEATS = 16384
N_FEAT = 4


def distinct_pick(key, take):
    groups_total = N_FEAT * N_FEAT
    scores = jax.random.randint(key, (groups_total, NB_DEV), 0, 1 << 20)
    order_ids = jnp.arange(NB_DEV, dtype=jnp.int32)[None, :]
    scores = scores * NB_DEV + order_ids
    chosen = jax.random.randint(jax.random.fold_in(key, 7), (), 0, groups_total)
    group_ids = jnp.arange(groups_total, dtype=jnp.int32)[:, None]
    scores = jnp.where((group_ids == chosen) & (order_ids == 0), -2, scores)
    scores = jnp.where((group_ids == chosen) & (order_ids == NB_DEV - 1), -1, scores)
    picked = jnp.argsort(scores, axis=1, stable=True)[:, :take].astype(jnp.int32)
    return picked.reshape(N_FEAT, N_FEAT, take)


def draw_panel_rows(key, part):
    key = jax.random.fold_in(key, 1)
    return distinct_pick(key, CAP)


def draw_pair_cols(key, part):
    key = jax.random.fold_in(key, 3)
    return distinct_pick(key, PPS)


def draw_pair_panel(key, part):
    key = jax.random.fold_in(key, 2)
    values = jax.random.randint(key, (N_FEAT, N_FEAT, PPS), 0, CAP)
    first_pos = jax.random.randint(jax.random.fold_in(key, 11), (N_FEAT, N_FEAT, 1), 0, PPS)
    second_pos = (first_pos + 1 + jax.random.randint(jax.random.fold_in(key, 12), (N_FEAT, N_FEAT, 1), 0, PPS - 1)) % PPS
    slot_ids = jnp.arange(PPS, dtype=jnp.int32)[None, None, :]
    values = jnp.where(slot_ids == first_pos, 0, values)
    values = jnp.where(slot_ids == second_pos, CAP - 1, values)
    return values.astype(jnp.int32)


def draw_pair_counts(key, part):
    key = jax.random.fold_in(key, 4)
    lowest = max(1, PPS // 3)
    counts = jax.random.randint(key, (N_FEAT, N_FEAT), lowest, PPS + 1)
    full_source = jax.random.randint(jax.random.fold_in(key, 21), (N_FEAT, 1), 0, N_FEAT)
    source_ids = jnp.arange(N_FEAT, dtype=jnp.int32)[None, :]
    counts = jnp.where(source_ids == full_source, PPS, counts)
    target_ids = jnp.arange(N_FEAT, dtype=jnp.int32)[:, None]
    chosen_d = jax.random.randint(jax.random.fold_in(key, 22), (), 0, N_FEAT)
    offset = jax.random.randint(jax.random.fold_in(key, 23), (), 1, N_FEAT)
    chosen_s = (jnp.sum(jnp.where(target_ids == chosen_d, full_source, 0)) + offset) % N_FEAT
    counts = jnp.where((target_ids == chosen_d) & (source_ids == chosen_s), lowest, counts)
    return counts.astype(jnp.int32)


def levels(rng, dims, cuts, smallest, high):
    level = 1.0
    for position, shards_of in cuts:
        steps = jax.random.uniform(jax.random.fold_in(jax.random.fold_in(rng, 6), position), (shards_of,), jnp.float32, smallest / len(cuts), high / len(cuts))
        level = level * jnp.repeat(jnp.exp(steps), dims[position] // shards_of).reshape((-1,) + (1,) * (len(dims) - 1 - position))
    return level


def normal_values(stream_key, shape, width, limit, split=(), kind=jnp.bfloat16):
    result = jax.random.normal(stream_key, shape, jnp.float32) * width
    if len(split) > 0:
        result = levels(stream_key, shape, split, -0.22, 0.18) * result
    return jnp.clip(result, min=-limit, max=limit).astype(kind)


def setup_inputs(seed: int = 0, part: int = 0) -> dict:
    seeds = jax.random.split(jax.random.key(seed), 7)
    part_keys = jax.random.split(jax.random.fold_in(seeds[6], part), 7)
    decoder = normal_values(part_keys[0], (FEATS, H), 1.0, 6.0, ((0, 4), (1, 4)))
    encoder = normal_values(part_keys[1], (H, FEATS), H ** -0.5, 0.09375, ((0, 4), (1, 4)))
    panel_rows = draw_panel_rows(jax.random.fold_in(jax.random.fold_in(seeds[6], part), 71), part)
    pair_panel = draw_pair_panel(jax.random.fold_in(jax.random.fold_in(seeds[6], part), 71), part)
    pair_cols = draw_pair_cols(jax.random.fold_in(jax.random.fold_in(seeds[6], part), 71), part)
    pair_counts = draw_pair_counts(jax.random.fold_in(jax.random.fold_in(seeds[6], part), 71), part)
    return dict(decoder=decoder, encoder=encoder, panel_rows=panel_rows, pair_panel=pair_panel, pair_cols=pair_cols, pair_counts=pair_counts)


def reference(decoder, encoder, panel_rows, pair_panel, pair_cols, pair_counts):
    source_ids = jnp.arange(N_FEAT, dtype=jnp.int32)[None, :, None]
    target_ids = jnp.arange(N_FEAT, dtype=jnp.int32)[:, None, None]
    local_row = jnp.take_along_axis(panel_rows, pair_panel, axis=2)
    row_index = (source_ids * NB_DEV + local_row).reshape(-1).astype(jnp.int32)
    col_index = (target_ids * NB_DEV + pair_cols).reshape(-1).astype(jnp.int32)
    slot_ids = jnp.arange(PPS, dtype=jnp.int32)[None, None, :]
    live = (slot_ids < pair_counts[:, :, None]).reshape(-1).astype(jnp.float32)

    def one_block(items):
        row_block, col_block, live_flag = items
        left_panel = lax.dynamic_slice_in_dim(decoder, row_block * BLK, BLK, 0)
        right_panel = lax.dynamic_slice_in_dim(encoder, col_block * BLK, BLK, 1)
        product = jnp.dot(left_panel, right_panel, preferred_element_type=jnp.float32)
        return product * live_flag

    return lax.map(one_block, (row_index, col_index, live))
```

```python
import functools

import jax
import jax.numpy as jnp
from jax import lax
from jax.experimental import pallas as pl
from jax.experimental.pallas import tpu as pltpu
from jax.sharding import PartitionSpec as P

BLK = 128
MESH = pl.DeviceIdType.MESH


def kernel(feats, hids, dec_hbm, enc_hbm, panel_v, panel_s, pick_s, cols_s, count_s, out_ref,
           dec, enc, stocks, outgoing, asked_v, asked_s, part, relay, extra,
           local_sem, strip_sem, ask_send, ask_recv, row_send, row_recv, z_send, z_recv, x_recv):
    pair = 2 if feats % 2 == 0 else 1
    tall = feats // pair
    groups = feats // hids
    cap = panel_s.shape[2]
    slots = pick_s.shape[2]
    step = part.shape[2]
    pieces = slots // step
    me, hid = lax.axis_index("feat"), lax.axis_index("hid")
    chip, core = me // pair, me % pair

    def target(k):
        return ((chip + k // pair) % tall) * pair + (core + k % pair) % pair

    def source(k):
        return ((chip + tall - k // pair) % tall) * pair + (core + pair - k % pair) % pair

    def back(k):
        return ((tall - k // pair) % tall) * pair + (pair - k % pair) % pair

    dec_copy = pltpu.make_async_copy(dec_hbm, dec, local_sem.at[0])
    dec_copy.start()

    def strip(c):
        col = pl.multiple_of(c * BLK, BLK)
        return pltpu.make_async_copy(enc_hbm.at[:, pl.ds(col, BLK)], enc.at[c], strip_sem.at[c])

    @pl.loop(0, enc.shape[0])
    def _(c):
        strip(c).start()

    barrier = pltpu.get_barrier_semaphore()

    @pl.loop(1, feats)
    def _(k):
        pl.semaphore_signal(barrier, inc=1, device_id={"feat": target(k)}, device_id_type=MESH)

    @pl.when(hid > 0)
    def _():
        pl.semaphore_signal(barrier, inc=1, device_id={"hid": hid - 1}, device_id_type=MESH)

    @pl.when(hid < hids - 1)
    def _():
        pl.semaphore_signal(barrier, inc=1, device_id={"hid": hid + 1}, device_id_type=MESH)

    lower = jnp.where(hid > 0, 1, 0)
    upper = jnp.where(hid < hids - 1, 1, 0)
    pl.semaphore_wait(barrier, feats - 1 + lower + upper)

    def ask(k):
        return pltpu.make_async_remote_copy(
            panel_v.at[0], asked_v.at[k], ask_send.at[k], ask_recv.at[k],
            device_id={"feat": target(k)}, device_id_type=MESH)

    def rows(k):
        return pltpu.make_async_remote_copy(
            outgoing.at[k], stocks[k], row_send.at[k], row_recv.at[k],
            device_id={"feat": target(k)}, device_id_type=MESH)

    @pl.loop(1, feats)
    def _(k):
        ask(k).start()

    dec_copy.wait()

    @pl.loop(1, feats)
    def _(k):
        ask(k).wait_recv()

    to_scalar = pltpu.make_async_copy(asked_v, asked_s, local_sem.at[1])
    to_scalar.start()
    to_scalar.wait()

    def ship(k):
        for j in range(cap):
            outgoing[k, j] = dec[asked_s[back(k), me, j]]
        rows(k).start()

    for k in list(range(pair, feats)) + list(range(1, pair)):
        ship(k)
    for j in range(cap):
        stocks[0][j] = dec[panel_s[0, me, j]]

    @pl.loop(0, enc.shape[0])
    def _(c):
        strip(c).wait()

    def pass_on(k, p, landing, sem, neighbour):
        return pltpu.make_async_remote_copy(
            part.at[k, p], landing, z_send.at[k, p], sem,
            device_id={"hid": neighbour}, device_id_type=MESH)

    def take_round(k):
        origin = source(k)
        owner = origin // groups
        mine = origin % groups

        if k > 0:
            rows(k).wait_recv()

        @pl.loop(0, pieces)
        def _(p):
            for i in range(step):
                slot = p * step + i
                live = jnp.minimum(jnp.maximum(count_s[0, origin] - slot, 0), 1)
                part[k, p, i] = live.astype(jnp.float32) * jnp.dot(
                    stocks[k][pick_s[0, origin, slot]], enc[cols_s[0, origin, slot]],
                    preferred_element_type=jnp.float32)

            @pl.when((hid > 0) & (hid <= owner))
            def _():
                pass_on(k, p, relay.at[k, p], z_recv.at[k, p], hid - 1).wait_recv()
                part[k, p] += relay[k, p]

            @pl.when((hid < hids - 1) & (hid > owner))
            def _():
                pass_on(k, p, relay.at[k, p], z_recv.at[k, p], hid + 1).wait_recv()
                part[k, p] += relay[k, p]

            @pl.when((hid < hids - 1) & (hid == owner))
            def _():
                pass_on(k, p, extra.at[mine, p], x_recv.at[mine, p], hid + 1).wait_recv()
                part[k, p] += extra[mine, p]

            @pl.when(hid < owner)
            def _():
                pass_on(k, p, relay.at[k, p], z_recv.at[k, p], hid + 1).start()

            @pl.when(hid > owner + 1)
            def _():
                pass_on(k, p, relay.at[k, p], z_recv.at[k, p], hid - 1).start()

            @pl.when(hid == owner + 1)
            def _():
                pass_on(k, p, extra.at[mine, p], x_recv.at[mine, p], hid - 1).start()

            @pl.when(hid == owner)
            def _():
                out_ref[pl.ds(mine * slots + p * step, step)] = part[k, p]

    for k in range(feats):
        take_round(k)

    for k in range(1, feats):
        ask(k).wait_send()
        rows(k).wait_send()

    @pl.loop(0, feats)
    def _(k):
        owner = source(k) // groups

        @pl.loop(0, pieces)
        def _(p):
            @pl.when(hid < owner)
            def _():
                pass_on(k, p, relay.at[k, p], z_recv.at[k, p], hid + 1).wait_send()

            @pl.when(hid > owner)
            def _():
                pass_on(k, p, relay.at[k, p], z_recv.at[k, p], hid - 1).wait_send()


def on_device(feats, hids, decoder, encoder, panel_rows, pair_panel, pair_cols, pair_counts):
    width = decoder.shape[1]
    blocks, strips = decoder.shape[0] // BLK, encoder.shape[1] // BLK
    cap = panel_rows.shape[2]
    slots = pair_panel.shape[2]
    step = 2 if slots % 2 == 0 else 1
    pieces = slots // step
    groups = feats // hids
    held = pl.BlockSpec(memory_space=pl.ANY)
    vector = pl.BlockSpec(memory_space=pltpu.VMEM)
    scalar = pl.BlockSpec(memory_space=pltpu.SMEM)
    dma = pltpu.SemaphoreType.DMA
    flops = 2 * feats * slots * BLK * BLK * width
    return pl.pallas_call(
        functools.partial(kernel, feats, hids),
        out_shape=jax.ShapeDtypeStruct((groups * slots, BLK, BLK), jnp.float32),
        in_specs=[held, held, vector, scalar, scalar, scalar, scalar],
        out_specs=vector,
        scratch_shapes=[
            pltpu.VMEM((blocks, BLK, width), decoder.dtype),
            pltpu.VMEM((strips, width, BLK), encoder.dtype),
            [pltpu.VMEM((cap, BLK, width), decoder.dtype) for _ in range(feats)],
            pltpu.VMEM((feats, cap, BLK, width), decoder.dtype),
            pltpu.VMEM((feats, feats, cap), jnp.int32),
            pltpu.SMEM((feats, feats, cap), jnp.int32),
            pltpu.VMEM((feats, pieces, step, BLK, BLK), jnp.float32),
            pltpu.VMEM((feats, pieces, step, BLK, BLK), jnp.float32),
            pltpu.VMEM((groups, pieces, step, BLK, BLK), jnp.float32),
            dma((2,)),
            dma((strips,)),
            dma((feats,)),
            dma((feats,)),
            dma((feats,)),
            dma((feats,)),
            dma((feats, pieces)),
            dma((feats, pieces)),
            dma((groups, pieces)),
        ],
        compiler_params=pltpu.CompilerParams(
            collective_id=0, has_side_effects=True, vmem_limit_bytes=60 * 1024 * 1024),
        cost_estimate=pl.CostEstimate(
            flops=flops, bytes_accessed=2 * decoder.size * 2, transcendentals=0),
    )(decoder.reshape(blocks, BLK, width), encoder, panel_rows, panel_rows, pair_panel, pair_cols, pair_counts)


def solution(mesh):
    placed = (
        P(("grp", "feat"), "hid"),
        P("hid", ("grp", "feat")),
        P(("grp", "feat"), None, None),
        P(("grp", "feat"), None, None),
        P(("grp", "feat"), None, None),
        P(("grp", "feat"), None),
    )
    return jax.shard_map(
        functools.partial(on_device, mesh.shape["feat"], mesh.shape["hid"]),
        mesh=mesh,
        in_specs=placed,
        out_specs=P(("grp", "feat", "hid"), None, None),
        check_vma=False,
    )
```

```python
import functools

import jax
import jax.numpy as jnp
from jax import lax
from jax.experimental import pallas as pl
from jax.experimental.pallas import tpu as pltpu
from jax.sharding import PartitionSpec as P

BLK = 128
CUTS = 2
MESH = pl.DeviceIdType.MESH


def kernel(feats, hids, dec_hbm, enc_hbm, panel_v, panel_s, pick_s, cols_s, count_s, out_ref,
           dec, enc, stocks, outgoing, asked_v, asked_s, part, relay, extra,
           local_sem, strip_sem, ask_send, ask_recv, row_send, row_recv, z_send, z_recv, x_recv):
    pair = 2 if feats % 2 == 0 else 1
    tall = feats // pair
    groups = feats // hids
    cap = panel_s.shape[2]
    slots = pick_s.shape[2]
    step = part.shape[2]
    sub = BLK // CUTS
    pieces = slots // step
    me, hid = lax.axis_index("feat"), lax.axis_index("hid")
    chip, core = me // pair, me % pair

    def target(k):
        return ((chip + k // pair) % tall) * pair + (core + k % pair) % pair

    def source(k):
        return ((chip + tall - k // pair) % tall) * pair + (core + pair - k % pair) % pair

    def back(k):
        return ((tall - k // pair) % tall) * pair + (pair - k % pair) % pair

    dec_copy = pltpu.make_async_copy(dec_hbm, dec, local_sem.at[0])
    dec_copy.start()

    def strip(c):
        col = pl.multiple_of(c * BLK, BLK)
        return pltpu.make_async_copy(enc_hbm.at[:, pl.ds(col, BLK)], enc.at[c], strip_sem.at[c])

    @pl.loop(0, enc.shape[0])
    def _(c):
        strip(c).start()

    barrier = pltpu.get_barrier_semaphore()

    @pl.loop(1, feats)
    def _(k):
        pl.semaphore_signal(barrier, inc=1, device_id={"feat": target(k)}, device_id_type=MESH)

    @pl.when(hid > 0)
    def _():
        pl.semaphore_signal(barrier, inc=1, device_id={"hid": hid - 1}, device_id_type=MESH)

    @pl.when(hid < hids - 1)
    def _():
        pl.semaphore_signal(barrier, inc=1, device_id={"hid": hid + 1}, device_id_type=MESH)

    lower = jnp.where(hid > 0, 1, 0)
    upper = jnp.where(hid < hids - 1, 1, 0)
    pl.semaphore_wait(barrier, feats - 1 + lower + upper)

    def ask(k):
        return pltpu.make_async_remote_copy(
            panel_v.at[0], asked_v.at[k], ask_send.at[k], ask_recv.at[k],
            device_id={"feat": target(k)}, device_id_type=MESH)

    def rows(k, h):
        q = k * CUTS + h
        return pltpu.make_async_remote_copy(
            outgoing.at[q], stocks[q], row_send.at[q], row_recv.at[q],
            device_id={"feat": target(k)}, device_id_type=MESH)

    @pl.loop(1, feats)
    def _(k):
        ask(k).start()

    dec_copy.wait()

    @pl.loop(1, feats)
    def _(k):
        ask(k).wait_recv()

    to_scalar = pltpu.make_async_copy(asked_v, asked_s, local_sem.at[1])
    to_scalar.start()
    to_scalar.wait()

    def ship(k):
        for h in range(CUTS):
            for j in range(cap):
                outgoing[k * CUTS + h, j] = dec[asked_s[back(k), me, j], h]
            rows(k, h).start()

    for k in list(range(pair, feats)) + list(range(1, pair)):
        ship(k)
    for j in range(cap):
        for h in range(CUTS):
            stocks[h][j] = dec[panel_s[0, me, j], h]

    @pl.loop(0, enc.shape[0])
    def _(c):
        strip(c).wait()

    def pass_on(k, p, landing, sem, neighbour):
        return pltpu.make_async_remote_copy(
            part.at[k, p], landing, z_send.at[k, p], sem,
            device_id={"hid": neighbour}, device_id_type=MESH)

    def take_round(k, h):
        q = k * CUTS + h
        origin = source(k)
        owner = origin // groups
        mine = origin % groups
        kept = mine * CUTS + h

        if k > 0:
            rows(k, h).wait_recv()

        @pl.loop(0, pieces)
        def _(p):
            for i in range(step):
                slot = p * step + i
                live = jnp.minimum(jnp.maximum(count_s[0, origin] - slot, 0), 1)
                part[q, p, i] = live.astype(jnp.float32) * jnp.dot(
                    stocks[q][pick_s[0, origin, slot]], enc[cols_s[0, origin, slot]],
                    preferred_element_type=jnp.float32)

            @pl.when((hid > 0) & (hid <= owner))
            def _():
                pass_on(q, p, relay.at[q, p], z_recv.at[q, p], hid - 1).wait_recv()
                part[q, p] += relay[q, p]

            @pl.when((hid < hids - 1) & (hid > owner))
            def _():
                pass_on(q, p, relay.at[q, p], z_recv.at[q, p], hid + 1).wait_recv()
                part[q, p] += relay[q, p]

            @pl.when((hid < hids - 1) & (hid == owner))
            def _():
                pass_on(q, p, extra.at[kept, p], x_recv.at[kept, p], hid + 1).wait_recv()
                part[q, p] += extra[kept, p]

            @pl.when(hid < owner)
            def _():
                pass_on(q, p, relay.at[q, p], z_recv.at[q, p], hid + 1).start()

            @pl.when(hid > owner + 1)
            def _():
                pass_on(q, p, relay.at[q, p], z_recv.at[q, p], hid - 1).start()

            @pl.when(hid == owner + 1)
            def _():
                pass_on(q, p, extra.at[kept, p], x_recv.at[kept, p], hid - 1).start()

            @pl.when(hid == owner)
            def _():
                out_ref[pl.ds(mine * slots + p * step, step), h * sub:(h + 1) * sub] = part[q, p]

    for k in range(feats):
        for h in range(CUTS):
            take_round(k, h)

    for k in range(1, feats):
        ask(k).wait_send()
        for h in range(CUTS):
            rows(k, h).wait_send()

    @pl.loop(0, feats * CUTS)
    def _(k):
        owner = source(k // CUTS) // groups

        @pl.loop(0, pieces)
        def _(p):
            @pl.when(hid < owner)
            def _():
                pass_on(k, p, relay.at[k, p], z_recv.at[k, p], hid + 1).wait_send()

            @pl.when(hid > owner)
            def _():
                pass_on(k, p, relay.at[k, p], z_recv.at[k, p], hid - 1).wait_send()


def on_device(feats, hids, decoder, encoder, panel_rows, pair_panel, pair_cols, pair_counts):
    width = decoder.shape[1]
    blocks, strips = decoder.shape[0] // BLK, encoder.shape[1] // BLK
    cap = panel_rows.shape[2]
    slots = pair_panel.shape[2]
    step = 2 if slots % 2 == 0 else 1
    pieces = slots // step
    groups = feats // hids
    sub = BLK // CUTS
    held = pl.BlockSpec(memory_space=pl.ANY)
    vector = pl.BlockSpec(memory_space=pltpu.VMEM)
    scalar = pl.BlockSpec(memory_space=pltpu.SMEM)
    dma = pltpu.SemaphoreType.DMA
    flops = 2 * feats * slots * BLK * BLK * width
    return pl.pallas_call(
        functools.partial(kernel, feats, hids),
        out_shape=jax.ShapeDtypeStruct((groups * slots, BLK, BLK), jnp.float32),
        in_specs=[held, held, vector, scalar, scalar, scalar, scalar],
        out_specs=vector,
        scratch_shapes=[
            pltpu.VMEM((blocks, CUTS, sub, width), decoder.dtype),
            pltpu.VMEM((strips, width, BLK), encoder.dtype),
            [pltpu.VMEM((cap, sub, width), decoder.dtype) for _ in range(feats * CUTS)],
            pltpu.VMEM((feats * CUTS, cap, sub, width), decoder.dtype),
            pltpu.VMEM((feats, feats, cap), jnp.int32),
            pltpu.SMEM((feats, feats, cap), jnp.int32),
            pltpu.VMEM((feats * CUTS, pieces, step, sub, BLK), jnp.float32),
            pltpu.VMEM((feats * CUTS, pieces, step, sub, BLK), jnp.float32),
            pltpu.VMEM((groups * CUTS, pieces, step, sub, BLK), jnp.float32),
            dma((2,)),
            dma((strips,)),
            dma((feats,)),
            dma((feats,)),
            dma((feats * CUTS,)),
            dma((feats * CUTS,)),
            dma((feats * CUTS, pieces)),
            dma((feats * CUTS, pieces)),
            dma((groups * CUTS, pieces)),
        ],
        compiler_params=pltpu.CompilerParams(
            collective_id=0, has_side_effects=True, vmem_limit_bytes=60 * 1024 * 1024),
        cost_estimate=pl.CostEstimate(
            flops=flops, bytes_accessed=2 * decoder.size * 2, transcendentals=0),
    )(decoder.reshape(blocks, CUTS, sub, width), encoder, panel_rows, panel_rows, pair_panel, pair_cols, pair_counts)


def solution(mesh):
    placed = (
        P(("grp", "feat"), "hid"),
        P("hid", ("grp", "feat")),
        P(("grp", "feat"), None, None),
        P(("grp", "feat"), None, None),
        P(("grp", "feat"), None, None),
        P(("grp", "feat"), None),
    )
    return jax.shard_map(
        functools.partial(on_device, mesh.shape["feat"], mesh.shape["hid"]),
        mesh=mesh,
        in_specs=placed,
        out_specs=P(("grp", "feat", "hid"), None, None),
        check_vma=False,
    )
```

```python
import functools

import jax
import jax.numpy as jnp
from jax import lax
from jax.experimental import pallas as pl
from jax.experimental.pallas import tpu as pltpu
from jax.sharding import PartitionSpec as P

BLK = 128
CUTS = 2
MESH = pl.DeviceIdType.MESH


def kernel(feats, hids, dec_hbm, enc_hbm, panel_v, panel_s, pick_s, cols_s, count_s, out_ref,
           dec, enc, stocks, outgoing, asked_v, asked_s, part, relay, extra,
           local_sem, strip_sem, ask_send, ask_recv, row_send, row_recv, z_send, z_recv, x_recv):
    pair = 2 if feats % 2 == 0 else 1
    tall = feats // pair
    groups = feats // hids
    cap = panel_s.shape[2]
    slots = pick_s.shape[2]
    step = part.shape[2]
    sub = BLK // CUTS
    pieces = slots // step
    me, hid = lax.axis_index("feat"), lax.axis_index("hid")
    chip, core = me // pair, me % pair

    def target(k):
        return ((chip + k // pair) % tall) * pair + (core + k % pair) % pair

    def source(k):
        return ((chip + tall - k // pair) % tall) * pair + (core + pair - k % pair) % pair

    def back(k):
        return ((tall - k // pair) % tall) * pair + (pair - k % pair) % pair

    dec_copy = pltpu.make_async_copy(dec_hbm, dec, local_sem.at[0])
    dec_copy.start()

    def strip(c):
        col = pl.multiple_of(c * BLK, BLK)
        return pltpu.make_async_copy(enc_hbm.at[:, pl.ds(col, BLK)], enc.at[c], strip_sem.at[c])

    @pl.loop(0, enc.shape[0])
    def _(c):
        strip(c).start()

    barrier = pltpu.get_barrier_semaphore()

    @pl.loop(1, feats)
    def _(k):
        pl.semaphore_signal(barrier, inc=1, device_id={"feat": target(k)}, device_id_type=MESH)

    @pl.when(hid > 0)
    def _():
        pl.semaphore_signal(barrier, inc=1, device_id={"hid": hid - 1}, device_id_type=MESH)

    @pl.when(hid < hids - 1)
    def _():
        pl.semaphore_signal(barrier, inc=1, device_id={"hid": hid + 1}, device_id_type=MESH)

    lower = jnp.where(hid > 0, 1, 0)
    upper = jnp.where(hid < hids - 1, 1, 0)
    pl.semaphore_wait(barrier, feats - 1 + lower + upper)

    def ask(k):
        return pltpu.make_async_remote_copy(
            panel_v.at[0], asked_v.at[k], ask_send.at[k], ask_recv.at[k],
            device_id={"feat": target(k)}, device_id_type=MESH)

    def rows(k, h):
        q = k * CUTS + h
        return pltpu.make_async_remote_copy(
            outgoing.at[q], stocks[q], row_send.at[q], row_recv.at[q],
            device_id={"feat": target(k)}, device_id_type=MESH)

    @pl.loop(1, feats)
    def _(k):
        ask(k).start()

    dec_copy.wait()

    @pl.loop(1, feats)
    def _(k):
        ask(k).wait_recv()

    to_scalar = pltpu.make_async_copy(asked_v, asked_s, local_sem.at[1])
    to_scalar.start()
    to_scalar.wait()

    def ship(k):
        for h in range(CUTS):
            for j in range(cap):
                outgoing[k * CUTS + h, j] = dec[asked_s[back(k), me, j], h]
            rows(k, h).start()

    for k in list(range(pair, feats)) + list(range(1, pair)):
        ship(k)
    for j in range(cap):
        for h in range(CUTS):
            stocks[h][j] = dec[panel_s[0, me, j], h]

    @pl.loop(0, enc.shape[0])
    def _(c):
        strip(c).wait()

    def pass_on(k, p, landing, sem, neighbour):
        return pltpu.make_async_remote_copy(
            part.at[k, p], landing, z_send.at[k, p], sem,
            device_id={"hid": neighbour}, device_id_type=MESH)

    def take_round(k, h):
        q = k * CUTS + h
        origin = source(k)
        owner = origin // groups
        mine = origin % groups
        kept = mine * CUTS + h

        inward = jnp.where(hid > owner, hids - 1 - hid, hid)
        lag = jnp.where(hid == owner, jnp.maximum(hid, hids - 1 - hid), inward)

        def take_piece(p):
            if k > 0:
                @pl.when(p == 0)
                def _():
                    rows(k, h).wait_recv()

            for i in range(step):
                slot = p * step + i
                live = jnp.minimum(jnp.maximum(count_s[0, origin] - slot, 0), 1)
                part[q, p, i] = live.astype(jnp.float32) * jnp.dot(
                    stocks[q][pick_s[0, origin, slot]], enc[cols_s[0, origin, slot]],
                    preferred_element_type=jnp.float32)

            @pl.when((hid > 0) & (hid <= owner))
            def _():
                pass_on(q, p, relay.at[q, p], z_recv.at[q, p], hid - 1).wait_recv()
                part[q, p] += relay[q, p]

            @pl.when((hid < hids - 1) & (hid > owner))
            def _():
                pass_on(q, p, relay.at[q, p], z_recv.at[q, p], hid + 1).wait_recv()
                part[q, p] += relay[q, p]

            @pl.when((hid < hids - 1) & (hid == owner))
            def _():
                pass_on(q, p, extra.at[kept, p], x_recv.at[kept, p], hid + 1).wait_recv()
                part[q, p] += extra[kept, p]

            @pl.when(hid < owner)
            def _():
                pass_on(q, p, relay.at[q, p], z_recv.at[q, p], hid + 1).start()

            @pl.when(hid > owner + 1)
            def _():
                pass_on(q, p, relay.at[q, p], z_recv.at[q, p], hid - 1).start()

            @pl.when(hid == owner + 1)
            def _():
                pass_on(q, p, extra.at[kept, p], x_recv.at[kept, p], hid - 1).start()

            @pl.when(hid == owner)
            def _():
                out_ref[pl.ds(mine * slots + p * step, step), h * sub:(h + 1) * sub] = part[q, p]

        return lag, take_piece

    turns = [take_round(k, h) for k in range(feats) for h in range(CUTS)]
    starts = [q * pieces for q in range(feats * CUTS)]

    @pl.loop(0, starts[-1] + pieces + hids - 1)
    def _(t):
        for q in range(feats * CUTS):
            lag, take_piece = turns[q]
            p = t - starts[q] - lag

            @pl.when((p >= 0) & (p < pieces))
            def _():
                take_piece(p)

    for k in range(1, feats):
        ask(k).wait_send()
        for h in range(CUTS):
            rows(k, h).wait_send()

    @pl.loop(0, feats * CUTS)
    def _(k):
        owner = source(k // CUTS) // groups

        @pl.loop(0, pieces)
        def _(p):
            @pl.when(hid < owner)
            def _():
                pass_on(k, p, relay.at[k, p], z_recv.at[k, p], hid + 1).wait_send()

            @pl.when(hid > owner)
            def _():
                pass_on(k, p, relay.at[k, p], z_recv.at[k, p], hid - 1).wait_send()


def on_device(feats, hids, decoder, encoder, panel_rows, pair_panel, pair_cols, pair_counts):
    width = decoder.shape[1]
    blocks, strips = decoder.shape[0] // BLK, encoder.shape[1] // BLK
    cap = panel_rows.shape[2]
    slots = pair_panel.shape[2]
    step = 2 if slots % 2 == 0 else 1
    pieces = slots // step
    groups = feats // hids
    sub = BLK // CUTS
    held = pl.BlockSpec(memory_space=pl.ANY)
    vector = pl.BlockSpec(memory_space=pltpu.VMEM)
    scalar = pl.BlockSpec(memory_space=pltpu.SMEM)
    dma = pltpu.SemaphoreType.DMA
    flops = 2 * feats * slots * BLK * BLK * width
    return pl.pallas_call(
        functools.partial(kernel, feats, hids),
        out_shape=jax.ShapeDtypeStruct((groups * slots, BLK, BLK), jnp.float32),
        in_specs=[held, held, vector, scalar, scalar, scalar, scalar],
        out_specs=vector,
        scratch_shapes=[
            pltpu.VMEM((blocks, CUTS, sub, width), decoder.dtype),
            pltpu.VMEM((strips, width, BLK), encoder.dtype),
            [pltpu.VMEM((cap, sub, width), decoder.dtype) for _ in range(feats * CUTS)],
            pltpu.VMEM((feats * CUTS, cap, sub, width), decoder.dtype),
            pltpu.VMEM((feats, feats, cap), jnp.int32),
            pltpu.SMEM((feats, feats, cap), jnp.int32),
            pltpu.VMEM((feats * CUTS, pieces, step, sub, BLK), jnp.float32),
            pltpu.VMEM((feats * CUTS, pieces, step, sub, BLK), jnp.float32),
            pltpu.VMEM((groups * CUTS, pieces, step, sub, BLK), jnp.float32),
            dma((2,)),
            dma((strips,)),
            dma((feats,)),
            dma((feats,)),
            dma((feats * CUTS,)),
            dma((feats * CUTS,)),
            dma((feats * CUTS, pieces)),
            dma((feats * CUTS, pieces)),
            dma((groups * CUTS, pieces)),
        ],
        compiler_params=pltpu.CompilerParams(
            collective_id=0, has_side_effects=True, vmem_limit_bytes=60 * 1024 * 1024),
        cost_estimate=pl.CostEstimate(
            flops=flops, bytes_accessed=2 * decoder.size * 2, transcendentals=0),
    )(decoder.reshape(blocks, CUTS, sub, width), encoder, panel_rows, panel_rows, pair_panel, pair_cols, pair_counts)


def solution(mesh):
    placed = (
        P(("grp", "feat"), "hid"),
        P("hid", ("grp", "feat")),
        P(("grp", "feat"), None, None),
        P(("grp", "feat"), None, None),
        P(("grp", "feat"), None, None),
        P(("grp", "feat"), None),
    )
    return jax.shard_map(
        functools.partial(on_device, mesh.shape["feat"], mesh.shape["hid"]),
        mesh=mesh,
        in_specs=placed,
        out_specs=P(("grp", "feat", "hid"), None, None),
        check_vma=False,
    )
```
